256 devices in a mesh: rep: 16 (over z_hi, x), fsdp: 16 (over y, z_lo, core).
Axes of the slice: x: 4, y: 4, z: 8 (z_hi: 4, z_lo: 2; z = z_hi * 2 + z_lo), core: 2. Of those that a mesh axis runs over, the one named last changes fastest.
Arguments:
- partial_grads: bfloat16 [256, 512, 8192], P(('rep', 'fsdp')), may hold values from -6 to 6
- momentum: float32 [8192, 8192], P('rep', 'fsdp'), may hold values from -6 to 6
- freq_index: int32 [16, 8, 128, 32], P('rep', None, 'fsdp'), may hold values from 0 to 4095, all different within a row
Outputs:
- new_momentum: float32 [8192, 8192], P('rep', 'fsdp')
- update: float32 [512, 8192], P(None, 'fsdp')
The draws below stay inside these ranges and needn't reach their ends.
Inputs may be any that keep to these rules, and one draw needn't show every extreme that they name: `freq_index`: the 32 frequencies of one block of one replica are distinct.
All inputs are finite; a program needn't handle non-finite values.
Results may differ from the reference program's by a relative error of at most 0.0003.
Values may be sent and summed in bfloat16 or wider, within the bound.
No kernel may reach another device: no remote copies, remote signals or barrier semaphores. Data moves between devices by JAX's collectives and lax.ppermute only.
A program may use at most 128 MiB of HBM per device.

```python
import jax
import jax.numpy as jnp
from jax import lax

D = 8192
ROWS = 512
GROUP = 64
K = 32
N_REP = 16
N_FSDP = 16


def with_spikes(entries, rng, source, target, shards_of, factor):
    owner, partner = [(jnp.arange(entries.shape[dim]) // (entries.shape[dim] // shards_of)).reshape([-1 if axis == dim else 1 for axis in range(entries.ndim)]) for dim in (source, target)]
    chosen = jax.random.permutation(rng, shards_of)[partner]
    strong = (owner == chosen) | (owner == (partner + shards_of // 2) % shards_of)
    return jnp.where(strong, factor * entries, entries)


def block_scale(own_key, shape, split, least, high):
    def one(dim, shards_of):
        heights = jax.random.uniform(jax.random.fold_in(jax.random.fold_in(own_key, 6), dim), (shards_of,), jnp.float32, least / len(split), high / len(split))
        return jnp.repeat(jnp.exp(heights), shape[dim] // shards_of).reshape((-1,) + (1,) * (len(shape) - dim - 1))

    gain = one(*split[0])
    for cut in split[1:]:
        gain = gain * one(*cut)
    return gain


def choose_distinct(rng, rows, number_of, top, lift):
    order = jax.random.permutation(jax.random.fold_in(rng, 1), number_of)
    boost = order
    for power in range(3):
        boost = boost * boost // number_of
    boost = boost * lift // number_of
    tickets = jax.random.randint(jax.random.fold_in(rng, 2), (rows, number_of), 0, 4096) + boost
    holders = jax.random.permutation(jax.random.fold_in(rng, 3), rows)[jnp.arange(number_of) % rows]
    tickets = jnp.where(jnp.arange(rows)[:, None] == holders[None, :], 1 << 14, tickets)
    priority = tickets * number_of + jnp.arange(number_of)
    return lax.top_k(priority.astype(jnp.int32), top)[1].astype(jnp.int32)


def normal_values(rng, dims, scale, bound, shards=(), held_as=jnp.bfloat16):
    entries = scale * jax.random.normal(rng, dims, jnp.float32)
    if shards:
        entries = entries * block_scale(rng, dims, shards, -0.22, 0.18)
    return jnp.clip(entries, -bound, bound).astype(held_as)


def noise_with(stream_key, shape, width, bound, shards, heavy, kind=jnp.bfloat16):
    result = width * jax.random.normal(stream_key, shape, jnp.float32)
    if shards:
        result = result * block_scale(stream_key, shape, shards, -0.22, 0.18)
    return jnp.clip(with_spikes(result, jax.random.fold_in(stream_key, 3), *heavy), -bound, bound).astype(kind)


def setup_inputs(seed: int = 0) -> dict:
    streams_of = jax.random.split(jax.random.key(seed), 4)
    return {
        "partial_grads": noise_with(streams_of[0], (N_REP * N_FSDP, ROWS, D), 0.5, 6.0, ((0, 256),), (0, 2, 256, 6.0)),
        "momentum": normal_values(streams_of[1], (N_REP * ROWS, D), 1.0, 6.0, ((0, 16), (1, 16)), jnp.float32),
        "freq_index": choose_distinct(streams_of[2], N_REP * (ROWS // GROUP) * (D // GROUP), GROUP * GROUP, K, 0).reshape((N_REP, ROWS // GROUP, D // GROUP, K)),
    }


momentum_decay = 0.9

def dct_basis(order):
    freq = jnp.arange(order, dtype=jnp.int32)[:, None]
    place = jnp.arange(order, dtype=jnp.int32)[None, :]
    phase = (2 * place + 1) * freq % (4 * order)
    scaling = jnp.where(freq == 0, jnp.sqrt(jnp.float32(1.0) / order), jnp.sqrt(jnp.float32(2.0) / order))
    return scaling * jnp.cos(jnp.pi * phase.astype(jnp.float32) / (2.0 * order))

def forward_blocks(field, basis, order):
    row_blocks = field.shape[0] // order
    col_blocks = field.shape[1] // order
    blocks = field.reshape(row_blocks, order, col_blocks, order)
    coef = jnp.einsum('kn,anbm,lm->abkl', basis, blocks, basis, precision=lax.Precision.HIGHEST)
    return coef.reshape(row_blocks, col_blocks, order * order)

def inverse_blocks(coef, basis, order):
    row_blocks, col_blocks = (coef.shape[0], coef.shape[1])
    square = coef.reshape(row_blocks, col_blocks, order, order)
    field = jnp.einsum('kn,abkl,lm->anbm', basis, square, basis, precision=lax.Precision.HIGHEST)
    return field.reshape(row_blocks * order, col_blocks * order)

def place_dense(values, positions, freqs):
    row_blocks, col_blocks = (values.shape[0], values.shape[1])
    row_ids = jnp.arange(row_blocks, dtype=jnp.int32)[:, None, None]
    col_ids = jnp.arange(col_blocks, dtype=jnp.int32)[None, :, None]
    empty = jnp.zeros((row_blocks, col_blocks, freqs), values.dtype)
    return empty.at[row_ids, col_ids, positions.astype(jnp.int32)].add(values)

def reference(partial_grads, momentum, freq_index):
    basis = dct_basis(GROUP)
    grads = partial_grads.astype(jnp.float32).reshape(N_REP, N_FSDP, ROWS, D).sum(axis=1)
    moment = momentum_decay * momentum.reshape(N_REP, ROWS, D) + grads

    def per_replica(pair):
        field, positions = pair
        coef = forward_blocks(field, basis, GROUP)
        kept = jnp.take_along_axis(coef, positions.astype(jnp.int32), axis=2)
        dense = place_dense(kept, positions, GROUP * GROUP)
        return (field - inverse_blocks(dense, basis, GROUP), dense)
    fresh, dense = lax.map(per_replica, (moment, freq_index))
    update = inverse_blocks(dense.sum(axis=0), basis, GROUP)
    return (fresh.reshape(N_REP * ROWS, D), update)
```

```python
import functools

import jax
import jax.numpy as jnp
import numpy as np
from jax import lax
from jax.experimental import pallas as pl
from jax.experimental.pallas import tpu as pltpu
from jax.sharding import PartitionSpec as P

GROUP = 64
K = 32
WIDE = 256
KEPT = 128
CHUNK = 128
DECAY = 0.9
BF = jnp.bfloat16
F32 = jnp.float32


def dct_constants():
    k = np.arange(GROUP)[:, None]
    n = np.arange(GROUP)[None, :]
    scale = np.where(k == 0, np.sqrt(1.0 / GROUP), np.sqrt(2.0 / GROUP))
    basis = scale * np.cos(np.pi * ((2 * n + 1) * k % (4 * GROUP)) / (2.0 * GROUP))
    wide = np.kron(np.eye(WIDE // GROUP), basis)
    both = np.stack([wide, wide.T]).astype(np.float32)
    high = both.astype(BF)
    low = (both - high.astype(np.float32)).astype(BF)
    return np.stack([high, low], axis=1)


def cut(x):
    high = x.astype(BF)
    return high, (x - high.astype(F32)).astype(BF)


def dot(a, b):
    return jnp.dot(a, b, preferred_element_type=F32)


def times_right(x, m_high, m_low):
    high, low = cut(x)
    return dot(high, m_high) + dot(high, m_low) + dot(low, m_high)


def times_left(m_high, m_low, x):
    high, low = cut(x)
    return dot(m_high, high) + dot(m_low, high) + dot(m_high, low)


def forward(field, basis):
    rows = field.shape[0]
    part = times_right(field, basis[1, 0], basis[1, 1])
    return times_left(basis[0, 0, :rows, :rows], basis[0, 1, :rows, :rows], part)


def inverse(coef, basis):
    rows = coef.shape[0]
    part = times_right(coef, basis[0, 0], basis[0, 1])
    return times_left(basis[1, 0, :rows, :rows], basis[1, 1, :rows, :rows], part)


def hits(pos):
    block = lax.broadcasted_iota(jnp.int32, (1, KEPT), 1) // K
    row = pos // GROUP
    col = pos % GROUP + block * GROUP
    on_row = lax.broadcasted_iota(jnp.int32, (GROUP, KEPT), 0) == row
    on_col = lax.broadcasted_iota(jnp.int32, (WIDE, KEPT), 0) == col
    return on_row, on_col


def one(mask):
    return jnp.where(mask, F32(1.0), F32(0.0)).astype(BF)


def by_lanes(a, b):
    return lax.dot_general(a, b, (((1,), (1,)), ((), ())), preferred_element_type=F32)


def by_rows(a, b):
    return lax.dot_general(a, b, (((0,), (0,)), ((), ())), preferred_element_type=F32)


def encode(field, pos_ref, basis, fresh_ref, kept_ref):
    rows, cols = field.shape
    for half in range(cols // WIDE):
        span = slice(half * WIDE, (half + 1) * WIDE)
        part = field[:, span]
        coef = forward(part, basis)
        dense = []
        for a in range(rows // GROUP):
            g = a * (cols // WIDE) + half
            block = coef[a * GROUP:(a + 1) * GROUP]
            on_row, on_col = hits(pos_ref[g:g + 1])
            row_one = one(on_row)
            chosen = by_lanes(row_one, one(on_col))
            dense.append(jnp.where(chosen > 0.5, block, F32(0.0)))
            high, low = cut(block)
            rest = (block - high.astype(F32) - low.astype(F32)).astype(BF)
            three = jnp.concatenate([high, low, rest], axis=0)
            rows_of = by_rows(three, jnp.concatenate([row_one] * 3, axis=0))
            kept_ref[g:g + 1] = jnp.sum(jnp.where(on_col, rows_of, F32(0.0)), axis=0, keepdims=True)
        fresh_ref[:, span] = part - inverse(jnp.concatenate(dense, axis=0), basis)


def encode_kernel(terms_ref, momentum_ref, pos_ref, basis_ref, fresh_ref, kept_ref):
    total = DECAY * momentum_ref[...]
    grad = terms_ref[0].astype(F32)
    for i in range(1, terms_ref.shape[0]):
        grad += terms_ref[i].astype(F32)
    encode(total + grad, pos_ref.at[0], basis_ref, fresh_ref, kept_ref.at[0])


def decode_kernel(*refs):
    n = (len(refs) - 2) // 2
    vals, poss = refs[:n], refs[n:2 * n]
    basis, out_ref = refs[2 * n:]
    groups = vals[0].shape[2]
    per_row = out_ref.shape[1] // WIDE
    for g in range(groups):
        left, right = [], []
        for val, pos in zip(vals, poss):
            for r in range(val.shape[0]):
                on_row, on_col = hits(pos[r, 0, g:g + 1])
                high, low = cut(jnp.where(on_row, val[r, 0, g:g + 1], F32(0.0)))
                left.append(jnp.concatenate([high, low], axis=0))
                right.append(one(on_col))
        both = by_lanes(jnp.concatenate(left, axis=1), jnp.concatenate(right, axis=1))
        field = inverse(both[:GROUP] + both[GROUP:], basis)
        a, half = g // per_row, g % per_row
        out_ref[a * GROUP:(a + 1) * GROUP, half * WIDE:(half + 1) * WIDE] = field


def across(n_hi, n_x, shift_hi, shift_x):
    return [
        (h * n_x + x, (h + shift_hi) % n_hi * n_x + (x + shift_x) % n_x)
        for h in range(n_hi)
        for x in range(n_x)
    ]


def gather_replicas(own):
    near = [own] + [lax.ppermute(own, "rep", across(4, 4, 0, s)) for s in (1, 2, 3)]
    near = jnp.stack(near)
    return [near] + [lax.ppermute(near, "rep", across(4, 4, s, 0)) for s in (1, 2, 3)]


def local(partial_grads, momentum, freq_index):
    rows, cols = momentum.shape
    n_fsdp = lax.axis_size("fsdp")
    chunks = rows // CHUNK
    groups = CHUNK // GROUP * (cols // WIDE)
    basis = jnp.asarray(dct_constants())
    pos = freq_index.reshape(chunks, groups, KEPT)
    pos_all = gather_replicas(pos)
    slab = partial_grads[0].reshape(rows, n_fsdp, cols).transpose(1, 0, 2)
    terms = lax.all_to_all(slab, "fsdp", 0, 0, tiled=True)
    params = pltpu.CompilerParams(vmem_limit_bytes=48 * 1024 * 1024)
    fresh, kept = pl.pallas_call(
        encode_kernel,
        grid=(chunks,),
        in_specs=[
            pl.BlockSpec((n_fsdp, CHUNK, cols), lambda i: (0, i, 0)),
            pl.BlockSpec((CHUNK, cols), lambda i: (i, 0)),
            pl.BlockSpec((1, groups, KEPT), lambda i: (i, 0, 0)),
            pl.BlockSpec(basis.shape, lambda i: (0, 0, 0, 0)),
        ],
        out_specs=[
            pl.BlockSpec((CHUNK, cols), lambda i: (i, 0)),
            pl.BlockSpec((1, groups, KEPT), lambda i: (i, 0, 0)),
        ],
        out_shape=[
            jax.ShapeDtypeStruct((rows, cols), F32),
            jax.ShapeDtypeStruct((chunks, groups, KEPT), F32),
        ],
        compiler_params=params,
        name="encode",
    )(terms, momentum, pos, basis)
    val_all = gather_replicas(kept)
    spec = pl.BlockSpec((4, 1, groups, KEPT), lambda i: (0, i, 0, 0))
    update = pl.pallas_call(
        decode_kernel,
        grid=(chunks,),
        in_specs=[spec] * 8 + [pl.BlockSpec(basis.shape, lambda i: (0, 0, 0, 0))],
        out_specs=pl.BlockSpec((CHUNK, cols), lambda i: (i, 0)),
        out_shape=jax.ShapeDtypeStruct((rows, cols), F32),
        compiler_params=params,
        name="decode",
    )(*val_all, *pos_all, basis)
    return fresh, update


def solution(mesh):
    return jax.shard_map(
        local,
        mesh=mesh,
        in_specs=(P(("rep", "fsdp"), None, None), P("rep", "fsdp"), P("rep", None, "fsdp", None)),
        out_specs=(P("rep", "fsdp"), P(None, "fsdp")),
        check_vma=False,
    )
```

```python
import functools

import jax
import jax.numpy as jnp
import numpy as np
from jax import lax
from jax.experimental import pallas as pl
from jax.experimental.pallas import tpu as pltpu
from jax.sharding import PartitionSpec as P

GROUP = 64
K = 32
WIDE = 256
KEPT = 128
CHUNK = 128
DECAY = 0.9
BF = jnp.bfloat16
F32 = jnp.float32


def dct_constants():
    k = np.arange(GROUP)[:, None]
    n = np.arange(GROUP)[None, :]
    scale = np.where(k == 0, np.sqrt(1.0 / GROUP), np.sqrt(2.0 / GROUP))
    basis = scale * np.cos(np.pi * ((2 * n + 1) * k % (4 * GROUP)) / (2.0 * GROUP))
    wide = np.kron(np.eye(WIDE // GROUP), basis)
    both = np.stack([wide, wide.T]).astype(np.float32)
    high = both.astype(BF)
    low = (both - high.astype(np.float32)).astype(BF)
    return np.stack([high, low], axis=1)


def cut(x):
    high = x.astype(BF)
    return high, (x - high.astype(F32)).astype(BF)


def dot(a, b):
    return jnp.dot(a, b, preferred_element_type=F32)


def times_right(x, m_high, m_low):
    high, low = cut(x)
    return dot(high, m_high) + dot(high, m_low) + dot(low, m_high)


def times_left(m_high, m_low, x):
    high, low = cut(x)
    return dot(m_high, high) + dot(m_low, high) + dot(m_high, low)


def down_rows(m, x):
    step = min(x.shape[0], 2 * GROUP)
    high, low = m[0, :step, :step], m[1, :step, :step]
    parts = [times_left(high, low, x[i:i + step]) for i in range(0, x.shape[0], step)]
    return jnp.concatenate(parts, axis=0) if len(parts) > 1 else parts[0]


def forward(field, basis):
    return down_rows(basis[0], times_right(field, basis[1, 0], basis[1, 1]))


def inverse(coef, basis):
    return down_rows(basis[1], times_right(coef, basis[0, 0], basis[0, 1]))


def match(places, count):
    return lax.broadcasted_iota(jnp.int32, (count, places.shape[1]), 0) == places


def one(mask):
    return jnp.where(mask, F32(1.0), F32(0.0)).astype(BF)


def by_lanes(a, b):
    return lax.dot_general(a, b, (((1,), (1,)), ((), ())), preferred_element_type=F32)


def by_rows(a, b):
    return lax.dot_general(a, b, (((0,), (0,)), ((), ())), preferred_element_type=F32)


def encode(field, pos_ref, basis, shift, fresh_ref, kept_ref):
    rows, cols = field.shape
    lane_block = lax.broadcasted_iota(jnp.int32, (1, KEPT), 1) // K
    per_group = KEPT // K
    kept = [None] * (rows // GROUP * (cols // WIDE))
    for half in range(cols // WIDE):
        span = slice(half * WIDE, (half + 1) * WIDE)
        part = field[:, span]
        coef = forward(part, basis)
        dense = []
        for a in range(rows // GROUP):
            g = a * (cols // WIDE) + half
            block = coef[a * GROUP:(a + 1) * GROUP]
            pos = pos_ref[g:g + 1]
            on_col = match(pos % GROUP + lane_block * GROUP, WIDE)
            row_one = one(match(pos // GROUP, GROUP))
            chosen = by_lanes(row_one, one(on_col))
            dense.append(jnp.where(chosen > 0.5, block, F32(0.0)))
            high, low = cut(block)
            rest = (block - high.astype(F32) - low.astype(F32)).astype(BF)
            three = jnp.concatenate([high, low, rest], axis=0)
            rows_of = by_rows(three, jnp.concatenate([row_one] * 3, axis=0))
            found = jnp.where(on_col, rows_of, F32(0.0))
            lines = []
            for q in range(per_group):
                line = jnp.sum(found[q * GROUP:(q + 1) * GROUP], axis=0, keepdims=True)
                lines.append(pltpu.roll(line, (KEPT - q * K) % KEPT, 1) if q else line)
            kept[g] = jnp.concatenate(lines, axis=0)
        fresh_ref[:, span] = part - inverse(jnp.concatenate(dense, axis=0), basis)
    kept = jnp.concatenate(kept, axis=0)
    kept_ref[...] = pltpu.roll(kept, shift, 1)


LEVELS = 32767.0
STEPS = 511.0
PAD = 16


def put(ref, x):
    if ref.dtype == F32:
        ref[...] = x
        return
    rows = x.shape[0]
    scale = jnp.maximum(jnp.ceil(jnp.max(jnp.abs(x), axis=0, keepdims=True) * STEPS), 1.0)
    ref[:rows] = jnp.round(x * (LEVELS * STEPS / scale)).astype(jnp.int32).astype(jnp.int16)
    ref[rows:] = jnp.broadcast_to(scale, (PAD, x.shape[1])).astype(jnp.int32).astype(jnp.int16)


def get(ref):
    if ref.dtype == F32:
        return ref[...]
    rows = ref.shape[0] - PAD
    scale = ref[rows:].astype(jnp.int32).astype(F32)[:1]
    return ref[:rows].astype(jnp.int32).astype(F32) * (scale * (1.0 / (LEVELS * STEPS)))


def pack_kernel(at_ref, *refs):
    for i in range(len(refs) // 2):
        refs[len(refs) // 2 + i][...] = refs[i][...]


def far_kernel(at_ref, own0, own1, sib_ref, up_ref, down_ref):
    put(up_ref, own0[0].astype(F32) + sib_ref[0].astype(F32))
    put(down_ref, own1[0].astype(F32) + sib_ref[1].astype(F32))


def near_kernel(at_ref, up0, up1, down0, down1, sib_up, sib_down, far_up, far_down, up_ref, down_ref):
    put(up_ref.at[0], up0[0].astype(F32) + sib_up[0].astype(F32) + get(far_up))
    put(up_ref.at[1], up1[0].astype(F32) + sib_up[1].astype(F32))
    put(down_ref.at[0], down0[0].astype(F32) + sib_down[0].astype(F32))
    put(down_ref.at[1], down1[0].astype(F32) + sib_down[1].astype(F32) + get(far_down))


def cross_kernel(at_ref, own0, own1, sib_ref, up_ref, down_ref, own_ref, out_ref):
    put(out_ref, own1[0].astype(F32) + sib_ref[1].astype(F32) + (get(up_ref.at[1]) + get(down_ref.at[1])))
    own_ref[...] = own0[0].astype(F32) + sib_ref[0].astype(F32) + (get(up_ref.at[0]) + get(down_ref.at[0]))


def encode_kernel(at_ref, own_ref, cross_ref, momentum_ref, pos_ref, basis_ref, *refs):
    *before, fresh_ref, kept_ref = refs
    field = DECAY * momentum_ref[...] + (own_ref[...] + get(cross_ref))
    first = 0
    for ref in before:
        kept_ref[first:first + ref.shape[0]] = ref[...]
        first += ref.shape[0]
    encode(field, pos_ref, basis_ref, at_ref[3] * K, fresh_ref, kept_ref.at[first:])


def decode_kernel(at_ref, *refs):
    *sent, basis, out_ref = refs
    count = len(sent) // 2
    vals, poss = sent[:count], sent[count:]
    per_row = out_ref.shape[1] // GROUP
    dense = []
    for i in range(vals[0].shape[0]):
        val = jnp.concatenate([ref[i:i + 1] for ref in vals], axis=1)
        pos = jnp.concatenate([ref[i:i + 1] for ref in poss], axis=1).astype(jnp.int32)
        high, low = cut(jnp.where(match(pos // GROUP, GROUP), val, F32(0.0)))
        both = by_lanes(jnp.concatenate([high, low], axis=0), one(match(pos % GROUP, GROUP)))
        dense.append(both[:GROUP] + both[GROUP:])
    wide = WIDE // GROUP
    for half in range(out_ref.shape[1] // WIDE):
        lines = [
            jnp.concatenate(dense[a + half * wide:a + (half + 1) * wide], axis=1)
            for a in range(0, len(dense), per_row)
        ]
        out_ref[:, half * WIDE:(half + 1) * WIDE] = inverse(jnp.concatenate(lines, axis=0), basis)


def across(n_hi, n_x, shift_hi, shift_x):
    return [
        (h * n_x + x, (h + shift_hi) % n_hi * n_x + (x + shift_x) % n_x)
        for h in range(n_hi)
        for x in range(n_x)
    ]


def along_x(own):
    return [own] + [lax.ppermute(own, "rep", across(4, 4, 0, s)) for s in (1, 2, 3)]


def along_z(near):
    return [near] + [lax.ppermute(near, "rep", across(4, 4, s, 0)) for s in (1, 2, 3)]


def places(shift_y, flip_z, flip_core):
    return [
        ((y * 2 + z) * 2 + c, ((y + shift_y) % 4 * 2 + (z ^ flip_z)) * 2 + (c ^ flip_core))
        for y in range(4)
        for z in range(2)
        for c in range(2)
    ]


def send(x, shift_y=0, flip_z=0, flip_core=0):
    return lax.ppermute(x, "fsdp", places(shift_y, flip_z, flip_core))


def piece(at, dy, dz, flip_core=0):
    return ((at[0] + dy) % 4 * 2 + (at[1] + dz) % 2) * 2 + (at[2] + flip_core) % 2


class Program:
    def __init__(self, at):
        self.at = at
        self.last = None

    def call(self, body, name, ins, outs, grid=(1,), onto=None):
        operands, specs = map(list, zip(*ins))
        count = len(operands)
        extra = [x for x in (onto, self.last) if x is not None]
        operands += extra
        specs += [pl.BlockSpec(memory_space=pl.ANY)] * len(extra)

        def kernel(at_ref, *refs):
            body(at_ref, *refs[:count], *refs[count + len(extra):])

        results = pl.pallas_call(
            kernel,
            grid_spec=pltpu.PrefetchScalarGridSpec(
                num_scalar_prefetch=1,
                grid=grid,
                in_specs=specs,
                out_specs=[spec for _, spec in outs],
            ),
            out_shape=[shape for shape, _ in outs],
            input_output_aliases={} if onto is None else {count + 1: 0},
            compiler_params=pltpu.CompilerParams(vmem_limit_bytes=VMEM),
            name=name,
        )(self.at, *operands)
        self.last = results[-1]
        return results


def whole(x):
    return x, pl.BlockSpec(x.shape, lambda s, at: (0,) * x.ndim)


class Chunk:
    def __init__(self, program, slab, start, rows, cols):
        self.program, self.call = program, program.call
        self.slab, self.rows, self.cols = slab, rows, cols
        self.start, self.index = start, start // rows

    def own(self, dy, dz):
        i, k = self.index, dy * 2 + dz
        return self.program.own, pl.BlockSpec((1, self.rows, self.cols), lambda s, at: (k, i, 0))

    def part(self, x, first, count):
        return x, pl.BlockSpec((count, *x.shape[1:]), lambda s, at: (first // count, 0, 0))

    def out(self, kind, *lead):
        shape = (*lead, self.rows + (0 if kind == F32 else PAD), self.cols)
        return jax.ShapeDtypeStruct(shape, kind), pl.BlockSpec(shape, lambda s, at: (0,) * len(shape))

    def pack(self, own_too):
        i, rows, cols, height = self.index, self.rows, self.cols, self.slab.shape[1]
        slab_spec = pl.BlockSpec((1, rows, cols), lambda s, at: (0, i, piece(at, s // 2, s % 2, 1)))
        out_spec = pl.BlockSpec((1, rows, cols), lambda s, at: (s, 0, 0))
        ins = [(self.slab, slab_spec)]
        outs = [(jax.ShapeDtypeStruct((8, rows, cols), BF), out_spec)]
        if own_too:
            ins.append((self.slab, pl.BlockSpec((1, height, cols), lambda s, at: (0, 0, piece(at, s // 2, s % 2)))))
            outs.append((jax.ShapeDtypeStruct((8, height, cols), BF),
                         pl.BlockSpec((1, height, cols), lambda s, at: (s, 0, 0))))
        packed, *own = self.call(pack_kernel, "pack", ins, outs, (8,))
        if own_too:
            self.program.own = own[0]
        self.sib = send(packed, flip_core=1)

    def far(self):
        up, down = self.call(
            far_kernel, "far", [self.own(2, 0), self.own(2, 1), self.part(self.sib, 4, 2)],
            [self.out(KINDS[0]), self.out(KINDS[0])],
        )
        self.far_up, self.far_down = send(up, shift_y=1), send(down, shift_y=-1)

    def near(self):
        up, down = self.call(
            near_kernel, "near",
            [self.own(1, 0), self.own(1, 1), self.own(3, 0), self.own(3, 1), self.part(self.sib, 2, 2),
             self.part(self.sib, 6, 2), whole(self.far_up), whole(self.far_down)],
            [self.out(KINDS[1], 2), self.out(KINDS[1], 2)],
        )
        self.up, self.down = send(up, shift_y=1), send(down, shift_y=-1)

    def cross(self):
        self.mine, cross = self.call(
            cross_kernel, "cross",
            [self.own(0, 0), self.own(0, 1), self.part(self.sib, 0, 2), whole(self.up), whole(self.down)],
            [self.out(F32), self.out(KINDS[2])],
        )
        self.crossed = send(cross, flip_z=1)

    def encode(self, momentum, pos, basis, onto, before):
        rows, cols, i = self.rows, self.cols, self.index
        groups = rows // GROUP * (cols // WIDE)
        first = self.start // GROUP * (cols // WIDE)
        pos = pos[first:first + groups]
        height = rows // GROUP * (cols // GROUP) + sum(x.shape[0] for x in before)
        self.fresh, self.kept = self.call(
            encode_kernel, "encode",
            [whole(self.mine), whole(self.crossed), (momentum, pl.BlockSpec((rows, cols), lambda s, at: (i, 0))),
             whole(pos), whole(basis), *map(whole, before)],
            [(jax.ShapeDtypeStruct(momentum.shape, F32), pl.BlockSpec((rows, cols), lambda s, at: (i, 0))),
             (jax.ShapeDtypeStruct((height, KEPT), F32), pl.BlockSpec((height, KEPT), lambda s, at: (0, 0)))],
            onto=onto,
        )


CHUNKS = (256, 256)
PLAN = "P0 P1 F0 F1 N0 N1 X0 E0 X1 E1 G0,1 D0,1"
KINDS = (jnp.int16,) * 3
VMEM = 16 * 1024 * 1024


STEP = 128


def local(partial_grads, momentum, freq_index):
    rows, cols = momentum.shape
    basis = jnp.asarray(dct_constants())
    pos = freq_index.reshape(rows // GROUP * (cols // WIDE), KEPT)
    me, rep = lax.axis_index("fsdp"), lax.axis_index("rep")
    at = jnp.stack([me // 4, me // 2 % 2, me % 2, rep % 4]).astype(jnp.int32)
    lines = jnp.tile(freq_index.reshape(rows // GROUP * (cols // GROUP), K).astype(F32), (1, KEPT // K))
    lines = jnp.where(jnp.arange(KEPT)[None] // K == rep % 4, lines, F32(0.0))
    program = Program(at)
    starts = np.cumsum((0,) + CHUNKS)[:-1]
    work = [Chunk(program, partial_grads, int(s), r, cols) for s, r in zip(starts, CHUNKS)]
    per_step = STEP // GROUP * (cols // GROUP)
    fresh = update = None
    before = [lines]
    for step in PLAN.split():
        kind, which = step[0], [work[int(i)] for i in step[1:].split(",")]
        chunk = which[0]
        if kind == "P":
            chunk.pack(chunk is work[-1])
        elif kind == "F":
            chunk.far()
        elif kind == "N":
            chunk.near()
        elif kind == "X":
            chunk.cross()
        elif kind == "E":
            chunk.encode(momentum, pos, basis, fresh, before)
            fresh, before = chunk.fresh, [chunk.kept]
        elif kind == "G":
            sent = along_z(sum(along_x(before[0])))
        else:
            first, steps = chunk.start // STEP, rows // STEP
            val_spec = pl.BlockSpec((per_step, KEPT), lambda s, at: (steps + first + s, 0))
            pos_spec = pl.BlockSpec((per_step, KEPT), lambda s, at: (first + s, 0))
            update, = program.call(
                decode_kernel, "decode",
                [(x, val_spec) for x in sent] + [(x, pos_spec) for x in sent] + [whole(basis)],
                [(jax.ShapeDtypeStruct((rows, cols), F32), pl.BlockSpec((STEP, cols), lambda s, at: (first + s, 0)))],
                (sum(c.rows for c in which) // STEP,),
                onto=update,
            )
    return fresh, update


def solution(mesh):
    return jax.shard_map(
        local,
        mesh=mesh,
        in_specs=(P(("rep", "fsdp"), None, None), P("rep", "fsdp"), P("rep", None, "fsdp", None)),
        out_specs=(P("rep", "fsdp"), P(None, "fsdp")),
        check_vma=False,
    )
```

```python
import functools

import jax
import jax.numpy as jnp
import numpy as np
from jax import lax
from jax.experimental import pallas as pl
from jax.experimental.pallas import tpu as pltpu
from jax.sharding import PartitionSpec as P

GROUP = 64
K = 32
WIDE = 256
KEPT = 128
CHUNK = 128
DECAY = 0.9
BF = jnp.bfloat16
F32 = jnp.float32


def dct_constants():
    k = np.arange(GROUP)[:, None]
    n = np.arange(GROUP)[None, :]
    scale = np.where(k == 0, np.sqrt(1.0 / GROUP), np.sqrt(2.0 / GROUP))
    basis = scale * np.cos(np.pi * ((2 * n + 1) * k % (4 * GROUP)) / (2.0 * GROUP))
    wide = np.kron(np.eye(WIDE // GROUP), basis)
    both = np.stack([wide, wide.T]).astype(np.float32)
    high = both.astype(BF)
    low = (both - high.astype(np.float32)).astype(BF)
    return np.stack([high, low], axis=1)


def cut(x):
    high = x.astype(BF)
    return high, (x - high.astype(F32)).astype(BF)


def dot(a, b):
    return jnp.dot(a, b, preferred_element_type=F32)


def times_right(x, m_high, m_low):
    high, low = cut(x)
    return dot(high, m_high) + dot(high, m_low) + dot(low, m_high)


def times_left(m_high, m_low, x):
    high, low = cut(x)
    return dot(m_high, high) + dot(m_low, high) + dot(m_high, low)


def down_rows(m, x):
    step = min(x.shape[0], 2 * GROUP)
    high, low = m[0, :step, :step], m[1, :step, :step]
    parts = [times_left(high, low, x[i:i + step]) for i in range(0, x.shape[0], step)]
    return jnp.concatenate(parts, axis=0) if len(parts) > 1 else parts[0]


def forward(field, basis):
    return down_rows(basis[0], times_right(field, basis[1, 0], basis[1, 1]))


def inverse(coef, basis):
    return down_rows(basis[1], times_right(coef, basis[0, 0], basis[0, 1]))


def match(places, count):
    return lax.broadcasted_iota(jnp.int32, (count, places.shape[1]), 0) == places


def one(mask):
    return jnp.where(mask, F32(1.0), F32(0.0)).astype(BF)


def by_lanes(a, b):
    return lax.dot_general(a, b, (((1,), (1,)), ((), ())), preferred_element_type=F32)


def by_rows(a, b):
    return lax.dot_general(a, b, (((0,), (0,)), ((), ())), preferred_element_type=F32)


def encode(field, pos_ref, basis, shift, fresh_ref, kept_ref):
    rows, cols = field.shape
    lane_block = lax.broadcasted_iota(jnp.int32, (1, KEPT), 1) // K
    per_group = KEPT // K
    kept = [None] * (rows // GROUP * (cols // WIDE))
    for half in range(cols // WIDE):
        span = slice(half * WIDE, (half + 1) * WIDE)
        part = field[:, span]
        coef = forward(part, basis)
        dense = []
        for a in range(rows // GROUP):
            g = a * (cols // WIDE) + half
            block = coef[a * GROUP:(a + 1) * GROUP]
            pos = pos_ref[g:g + 1]
            on_col = match(pos % GROUP + lane_block * GROUP, WIDE)
            row_one = one(match(pos // GROUP, GROUP))
            chosen = by_lanes(row_one, one(on_col))
            dense.append(jnp.where(chosen > 0.5, block, F32(0.0)))
            high, low = cut(block)
            rest = (block - high.astype(F32) - low.astype(F32)).astype(BF)
            three = jnp.concatenate([high, low, rest], axis=0)
            rows_of = by_rows(three, jnp.concatenate([row_one] * 3, axis=0))
            found = jnp.where(on_col, rows_of, F32(0.0))
            lines = []
            for q in range(per_group):
                line = jnp.sum(found[q * GROUP:(q + 1) * GROUP], axis=0, keepdims=True)
                lines.append(pltpu.roll(line, (KEPT - q * K) % KEPT, 1) if q else line)
            kept[g] = jnp.concatenate(lines, axis=0)
        fresh_ref[:, span] = part - inverse(jnp.concatenate(dense, axis=0), basis)
    kept = jnp.concatenate(kept, axis=0)
    kept_ref[...] = pltpu.roll(kept, shift, 1)


LEVELS = 32767.0
STEPS = 511.0
PAD = 16


def put(ref, x):
    if ref.dtype == F32:
        ref[...] = x
        return
    rows = x.shape[0]
    scale = jnp.maximum(jnp.ceil(jnp.max(jnp.abs(x), axis=0, keepdims=True) * STEPS), 1.0)
    ref[:rows] = jnp.round(x * (LEVELS * STEPS / scale)).astype(jnp.int32).astype(jnp.int16)
    ref[rows:] = jnp.broadcast_to(scale, (PAD, x.shape[1])).astype(jnp.int32).astype(jnp.int16)


def get(ref):
    if ref.dtype == F32:
        return ref[...]
    rows = ref.shape[0] - PAD
    scale = ref[rows:].astype(jnp.int32).astype(F32)[:1]
    return ref[:rows].astype(jnp.int32).astype(F32) * (scale * (1.0 / (LEVELS * STEPS)))


def wide(*refs):
    return sum(ref[0].astype(F32) for ref in refs)


def pack_kernel(at_ref, *refs):
    for i in range(len(refs) // 2):
        refs[len(refs) // 2 + i][...] = refs[i][...]


def far_kernel(at_ref, own, sib, up_ref, down_ref):
    x = wide(own, sib)
    put(up_ref, x[:HALF])
    put(down_ref, x[HALF:])


def near_kernel(at_ref, own_up, sib_up, own_down, sib_down, far_up, far_down, up_ref, down_ref):
    up, down = wide(own_up, sib_up), wide(own_down, sib_down)
    put(up_ref, jnp.concatenate([up[:HALF] + get(far_up), up[HALF:]], axis=0))
    put(down_ref, jnp.concatenate([down[:HALF], down[HALF:] + get(far_down)], axis=0))


def near_top_kernel(at_ref, own_up, sib_up, own_down, sib_down, far_up, momentum, basis, up_ref, down_ref, decayed, held):
    put(up_ref, wide(own_up, sib_up) + get(far_up))
    put(down_ref, wide(own_down, sib_down))
    decayed[...] = DECAY * momentum[...]
    held[...] = basis[...]


def near_low_kernel(at_ref, own_up, sib_up, own_down, sib_down, far_down, up_ref, down_ref):
    put(up_ref, wide(own_up, sib_up))
    put(down_ref, wide(own_down, sib_down) + get(far_down))


def cross_kernel(at_ref, own, sib, up_ref, down_ref, top_ref, low_ref):
    x = wide(own, sib) + (get(up_ref) + get(down_ref))
    put(top_ref, x[:HALF])
    put(low_ref, x[HALF:])


def encode_kernel(at_ref, own, sib, up_ref, down_ref, cross_ref, momentum_ref, pos_ref, basis_ref, *refs):
    *before, fresh_ref, kept_ref = refs
    field = momentum_ref[...] + (wide(own, sib) + (get(up_ref) + get(down_ref)) + get(cross_ref))
    first = 0
    for ref in before:
        kept_ref[first:first + ref.shape[0]] = ref[...]
        first += ref.shape[0]
    encode(field, pos_ref, basis_ref, at_ref[3] * K, fresh_ref, kept_ref.at[first:])


def decode_kernel(at_ref, *refs):
    *sent, basis, out_ref = refs
    count = len(sent) // 2
    vals, poss = sent[:count], sent[count:]
    per_row = out_ref.shape[1] // GROUP
    dense = []
    for i in range(vals[0].shape[0]):
        val = jnp.concatenate([ref[i:i + 1] for ref in vals], axis=1)
        pos = jnp.concatenate([ref[i:i + 1] for ref in poss], axis=1).astype(jnp.int32)
        high, low = cut(jnp.where(match(pos // GROUP, GROUP), val, F32(0.0)))
        both = by_lanes(jnp.concatenate([high, low], axis=0), one(match(pos % GROUP, GROUP)))
        dense.append(both[:GROUP] + both[GROUP:])
    wide = WIDE // GROUP
    for half in range(out_ref.shape[1] // WIDE):
        lines = [
            jnp.concatenate(dense[a + half * wide:a + (half + 1) * wide], axis=1)
            for a in range(0, len(dense), per_row)
        ]
        out_ref[:, half * WIDE:(half + 1) * WIDE] = inverse(jnp.concatenate(lines, axis=0), basis)


def across(n_hi, n_x, shift_hi, shift_x):
    return [
        (h * n_x + x, (h + shift_hi) % n_hi * n_x + (x + shift_x) % n_x)
        for h in range(n_hi)
        for x in range(n_x)
    ]


def along_x(own):
    return [own] + [lax.ppermute(own, "rep", across(4, 4, 0, s)) for s in (1, 2, 3)]


def along_z(near):
    return [near] + [lax.ppermute(near, "rep", across(4, 4, s, 0)) for s in (1, 2, 3)]


def places(shift_y, flip_z, flip_core):
    return [
        ((y * 2 + z) * 2 + c, ((y + shift_y) % 4 * 2 + (z ^ flip_z)) * 2 + (c ^ flip_core))
        for y in range(4)
        for z in range(2)
        for c in range(2)
    ]


def send(x, shift_y=0, flip_z=0, flip_core=0):
    return lax.ppermute(x, "fsdp", places(shift_y, flip_z, flip_core))


def piece(at, dy, dz, flip_core=0):
    return ((at[0] + dy) % 4 * 2 + (at[1] + dz) % 2) * 2 + (at[2] + flip_core) % 2


class Program:

    def __init__(self, at):
        self.at = at
        self.last = []

    def call(self, body, name, ins, outs, grid=(1,), onto=None):
        operands, specs = map(list, zip(*ins))
        count = len(operands)
        extra = ([] if onto is None else [onto]) + self.last
        operands += extra
        specs += [pl.BlockSpec(memory_space=pl.ANY)] * len(extra)

        def kernel(at_ref, *refs):
            body(at_ref, *refs[:count], *refs[count + len(extra):])

        results = pl.pallas_call(
            kernel,
            grid_spec=pltpu.PrefetchScalarGridSpec(
                num_scalar_prefetch=1,
                grid=grid,
                in_specs=specs,
                out_specs=[spec for _, spec in outs],
            ),
            out_shape=[shape for shape, _ in outs],
            input_output_aliases={} if onto is None else {count + 1: 0},
            compiler_params=pltpu.CompilerParams(vmem_limit_bytes=VMEM),
            name=name,
        )(self.at, *operands)
        self.last = [results[-1]]
        return results


def whole(x):
    return x, pl.BlockSpec(x.shape, lambda s, at: (0,) * x.ndim)


HALF = 256
SENT = jnp.int16
VMEM = 16 * 1024 * 1024


STEP = 128


def local(partial_grads, momentum, freq_index):
    rows, cols = momentum.shape
    basis = jnp.asarray(dct_constants())
    pos = freq_index.reshape(rows // GROUP * (cols // WIDE), KEPT)
    me, rep = lax.axis_index("fsdp"), lax.axis_index("rep")
    at = jnp.stack([me // 4, me // 2 % 2, me % 2, rep % 4]).astype(jnp.int32)
    lines = jnp.tile(freq_index.reshape(rows // GROUP * (cols // GROUP), K).astype(F32), (1, KEPT // K))
    lines = jnp.where(jnp.arange(KEPT)[None] // K == rep % 4, lines, F32(0.0))
    groups = HALF // GROUP * (cols // WIDE)
    poss = [pos[i * groups:(i + 1) * groups] for i in range(rows // HALF)]
    program = Program(at)
    call = program.call
    quarter = jax.ShapeDtypeStruct((4, rows, cols), BF)

    def slab(dz, flip_core):
        return partial_grads, pl.BlockSpec((1, rows, cols), lambda s, at: (0, 0, piece(at, s, dz, flip_core)))

    def packed():
        return quarter, pl.BlockSpec((1, rows, cols), lambda s, at: (s, 0, 0))

    def out(height):
        shape = (height + (0 if SENT == F32 else PAD), cols)
        return jax.ShapeDtypeStruct(shape, SENT), pl.BlockSpec(shape, lambda s, at: (0, 0))

    def like(x):
        return jax.ShapeDtypeStruct(x.shape, x.dtype), whole(x)[1]

    own, sib = {}, {}
    other, = call(pack_kernel, "pack", [slab(1, 1)], [packed()], (4,))
    sib[1] = send(other, flip_core=1)
    other, own[1], own[0] = call(
        pack_kernel, "pack", [slab(0, 1), slab(1, 0), slab(0, 0)], [packed(), packed(), packed()], (4,))
    sib[0] = send(other, flip_core=1)

    def both(dz, dy, height=rows, i=0):
        spec = pl.BlockSpec((1, height, cols), lambda s, at: (dy % 4, i, 0))
        return [(own[dz], spec), (sib[dz], spec)]

    def round_y(x):
        return send(x[0], shift_y=1), send(x[1], shift_y=-1)

    far = {}
    for dz in (1, 0):
        far[dz] = round_y(call(far_kernel, "far", both(dz, 2), [out(HALF)] * 2))
        if dz:
            program.last += [lines, *poss]
    across_near = round_y(call(
        near_kernel, "near", both(1, 1) + both(1, -1) + [whole(far[1][0]), whole(far[1][1])], [out(rows)] * 2))
    *top, decayed, held = call(
        near_top_kernel, "near",
        both(0, 1, HALF, 0) + both(0, -1, HALF, 0) + [whole(far[0][0]), whole(momentum), whole(basis)],
        [out(HALF)] * 2 + [like(momentum), like(basis)])
    near = [round_y(top)]
    crossing = call(
        cross_kernel, "cross", both(1, 0) + [whole(across_near[0]), whole(across_near[1])], [out(HALF)] * 2)
    crossed = [send(x, flip_z=1) for x in crossing]
    near.append(round_y(call(
        near_low_kernel, "near", both(0, 1, HALF, 1) + both(0, -1, HALF, 1) + [whole(far[0][1])], [out(HALF)] * 2)))
    fresh, kept = None, lines
    for i in range(rows // HALF):
        height = kept.shape[0] + HALF // GROUP * (cols // GROUP)
        half_spec = pl.BlockSpec((HALF, cols), lambda s, at, i=i: (i, 0))
        fresh, kept = call(
            encode_kernel, "encode",
            [*both(0, 0, HALF, i), whole(near[i][0]), whole(near[i][1]), whole(crossed[i]), (decayed, half_spec),
             whole(poss[i]), whole(held), whole(kept)],
            [(jax.ShapeDtypeStruct((rows, cols), F32), half_spec),
             (jax.ShapeDtypeStruct((height, KEPT), F32), pl.BlockSpec((height, KEPT), lambda s, at: (0, 0)))],
            onto=fresh,
        )
    sent = along_z(sum(along_x(kept)))
    per_step, steps = STEP // GROUP * (cols // GROUP), rows // STEP
    val_spec = pl.BlockSpec((per_step, KEPT), lambda s, at: (steps + s, 0))
    pos_spec = pl.BlockSpec((per_step, KEPT), lambda s, at: (s, 0))
    update, = call(
        decode_kernel, "decode",
        [(x, val_spec) for x in sent] + [(x, pos_spec) for x in sent] + [whole(held)],
        [(jax.ShapeDtypeStruct((rows, cols), F32), pl.BlockSpec((STEP, cols), lambda s, at: (s, 0)))],
        (steps,),
    )
    return fresh, update


def solution(mesh):
    return jax.shard_map(
        local,
        mesh=mesh,
        in_specs=(P(("rep", "fsdp"), None, None), P("rep", "fsdp"), P("rep", None, "fsdp", None)),
        out_specs=(P("rep", "fsdp"), P(None, "fsdp")),
        check_vma=False,
    )
```

```python
import functools

import jax
import jax.numpy as jnp
import numpy as np
from jax import lax
from jax.experimental import pallas as pl
from jax.experimental.pallas import tpu as pltpu
from jax.sharding import PartitionSpec as P

GROUP = 64
K = 32
WIDE = 256
KEPT = 128
CHUNK = 128
DECAY = 0.9
BF = jnp.bfloat16
F32 = jnp.float32


def dct_constants():
    k = np.arange(GROUP)[:, None]
    n = np.arange(GROUP)[None, :]
    scale = np.where(k == 0, np.sqrt(1.0 / GROUP), np.sqrt(2.0 / GROUP))
    basis = scale * np.cos(np.pi * ((2 * n + 1) * k % (4 * GROUP)) / (2.0 * GROUP))
    wide = np.kron(np.eye(WIDE // GROUP), basis)
    both = np.stack([wide, wide.T]).astype(np.float32)
    high = both.astype(BF)
    low = (both - high.astype(np.float32)).astype(BF)
    return np.stack([high, low], axis=1)


def cut(x):
    high = x.astype(BF)
    return high, (x - high.astype(F32)).astype(BF)


def dot(a, b):
    return jnp.dot(a, b, preferred_element_type=F32)


def times_right(x, m_high, m_low):
    high, low = cut(x)
    return dot(high, m_high) + dot(high, m_low) + dot(low, m_high)


def times_left(m_high, m_low, x):
    high, low = cut(x)
    return dot(m_high, high) + dot(m_low, high) + dot(m_high, low)


def down_rows(m, x):
    step = min(x.shape[0], 2 * GROUP)
    high, low = m[0, :step, :step], m[1, :step, :step]
    parts = [times_left(high, low, x[i:i + step]) for i in range(0, x.shape[0], step)]
    return jnp.concatenate(parts, axis=0) if len(parts) > 1 else parts[0]


def forward(field, basis):
    return down_rows(basis[0], times_right(field, basis[1, 0], basis[1, 1]))


def inverse(coef, basis):
    return down_rows(basis[1], times_right(coef, basis[0, 0], basis[0, 1]))


def match(places, count):
    return lax.broadcasted_iota(jnp.int32, (count, places.shape[1]), 0) == places


def one(mask):
    return jnp.where(mask, F32(1.0), F32(0.0)).astype(BF)


def by_lanes(a, b):
    return lax.dot_general(a, b, (((1,), (1,)), ((), ())), preferred_element_type=F32)


def by_rows(a, b):
    return lax.dot_general(a, b, (((0,), (0,)), ((), ())), preferred_element_type=F32)


def encode(field, pos_ref, basis, fresh_ref, kept_ref):
    rows, cols = field.shape
    lane_block = lax.broadcasted_iota(jnp.int32, (1, KEPT), 1) // K
    for half in range(cols // WIDE):
        span = slice(half * WIDE, (half + 1) * WIDE)
        part = field[:, span]
        coef = forward(part, basis)
        dense = []
        for a in range(rows // GROUP):
            g = a * (cols // WIDE) + half
            block = coef[a * GROUP:(a + 1) * GROUP]
            pos = pos_ref[g:g + 1]
            on_col = match(pos % GROUP + lane_block * GROUP, WIDE)
            row_one = one(match(pos // GROUP, GROUP))
            chosen = by_lanes(row_one, one(on_col))
            dense.append(jnp.where(chosen > 0.5, block, F32(0.0)))
            high, low = cut(block)
            rest = (block - high.astype(F32) - low.astype(F32)).astype(BF)
            three = jnp.concatenate([high, low, rest], axis=0)
            rows_of = by_rows(three, jnp.concatenate([row_one] * 3, axis=0))
            found = jnp.where(on_col, rows_of, F32(0.0))
            kept_ref[g:g + 1] = jnp.sum(found, axis=0, keepdims=True)
        fresh_ref[:, span] = part - inverse(jnp.concatenate(dense, axis=0), basis)


LEVELS = 32767.0
STEPS = 511.0
PAD = 16


def put(ref, x):
    if ref.dtype == F32:
        ref[...] = x
        return
    rows = x.shape[0]
    scale = jnp.maximum(jnp.ceil(jnp.max(jnp.abs(x), axis=0, keepdims=True) * STEPS), 1.0)
    ref[:rows] = jnp.round(x * (LEVELS * STEPS / scale)).astype(jnp.int32).astype(jnp.int16)
    ref[rows:] = jnp.broadcast_to(scale, (PAD, x.shape[1])).astype(jnp.int32).astype(jnp.int16)


def get(ref):
    if ref.dtype == F32:
        return ref[...]
    rows = ref.shape[0] - PAD
    scale = ref[rows:].astype(jnp.int32).astype(F32)[:1]
    return ref[:rows].astype(jnp.int32).astype(F32) * (scale * (1.0 / (LEVELS * STEPS)))


def wide(*refs):
    return sum(ref[0].astype(F32) for ref in refs)


def pack_kernel(at_ref, *refs):
    for i in range(len(refs) // 2):
        refs[len(refs) // 2 + i][...] = refs[i][...]


def far_kernel(at_ref, own, sib, up_ref, down_ref):
    x = wide(own, sib)
    put(up_ref, x[:HALF])
    put(down_ref, x[HALF:])


def near_kernel(at_ref, own_up, sib_up, own_down, sib_down, far_up, far_down, up_ref, down_ref):
    up, down = wide(own_up, sib_up), wide(own_down, sib_down)
    put(up_ref, jnp.concatenate([up[:HALF] + get(far_up), up[HALF:]], axis=0))
    put(down_ref, jnp.concatenate([down[:HALF], down[HALF:] + get(far_down)], axis=0))


def near_top_kernel(at_ref, own_up, sib_up, own_down, sib_down, far_up, momentum, basis, up_ref, down_ref, decayed, held):
    put(up_ref, wide(own_up, sib_up) + get(far_up))
    put(down_ref, wide(own_down, sib_down))
    decayed[...] = DECAY * momentum[...]
    held[...] = basis[...]


def near_low_kernel(at_ref, own_up, sib_up, own_down, sib_down, far_down, up_ref, down_ref):
    put(up_ref, wide(own_up, sib_up))
    put(down_ref, wide(own_down, sib_down) + get(far_down))


def cross_kernel(at_ref, own, sib, up_ref, down_ref, top_ref, low_ref):
    x = wide(own, sib) + (get(up_ref) + get(down_ref))
    put(top_ref, x[:HALF])
    put(low_ref, x[HALF:])


def encode_kernel(at_ref, own, sib, up_ref, down_ref, cross_ref, momentum_ref, pos_ref, basis_ref, *refs):
    *before, fresh_ref, kept_ref = refs
    field = momentum_ref[...] + (wide(own, sib) + (get(up_ref) + get(down_ref)) + get(cross_ref))
    first = 0
    for ref in before:
        kept_ref[first:first + ref.shape[0]] = ref[...]
        first += ref.shape[0]
    encode(field, pos_ref, basis_ref, fresh_ref, kept_ref.at[first:])


def spread_kernel(at_ref, *refs):
    *sent, out_ref = refs
    lane_block = lax.broadcasted_iota(jnp.int32, (1, KEPT), 1) // K
    groups = out_ref.shape[1]
    for q in range(KEPT // K):
        total = None
        for s in range(2 * len(sent)):
            part = jnp.where(lane_block == q, sent[s // 2][s % 2], F32(0.0))
            shift = (s - q) * K % KEPT
            part = pltpu.roll(part, shift, 1) if shift else part
            total = part if total is None else total + part
        out_ref[2 * q] = total[:groups]
        out_ref[2 * q + 1] = total[groups:]


def decode_kernel(at_ref, *refs):
    *sent, basis, out_ref = refs
    halves = out_ref.shape[1] // WIDE
    for half in range(halves):
        lines = []
        for g in range(half, sent[0].shape[1], halves):
            dense = []
            for q in range(WIDE // GROUP):
                pos = jnp.concatenate([ref[2 * q, g:g + 1] for ref in sent], axis=1).astype(jnp.int32)
                val = jnp.concatenate([ref[2 * q + 1, g:g + 1] for ref in sent], axis=1)
                high, low = cut(jnp.where(match(pos // GROUP, GROUP), val, F32(0.0)))
                both = by_lanes(jnp.concatenate([high, low], axis=0), one(match(pos % GROUP, GROUP)))
                dense.append(both[:GROUP] + both[GROUP:])
            lines.append(jnp.concatenate(dense, axis=1))
        out_ref[:, half * WIDE:(half + 1) * WIDE] = inverse(jnp.concatenate(lines, axis=0), basis)


def across(n_hi, n_x, shift_hi, shift_x):
    return [
        (h * n_x + x, (h + shift_hi) % n_hi * n_x + (x + shift_x) % n_x)
        for h in range(n_hi)
        for x in range(n_x)
    ]


def along_x(own):
    return [own] + [lax.ppermute(own, "rep", across(4, 4, 0, s)) for s in (1, 2, 3)]


def along_z(own):
    there = lax.ppermute(own, "rep", [(h * 4 + x, (h ^ 1) * 4 + x) for h in range(4) for x in range(4)])
    two = jnp.stack([own, there])
    return [two, lax.ppermute(two, "rep", [(h * 4 + x, (3 - h) * 4 + x) for h in range(4) for x in range(4)])]


def places(shift_y, flip_z, flip_core):
    return [
        ((y * 2 + z) * 2 + c, ((y + shift_y) % 4 * 2 + (z ^ flip_z)) * 2 + (c ^ flip_core))
        for y in range(4)
        for z in range(2)
        for c in range(2)
    ]


def send(x, shift_y=0, flip_z=0, flip_core=0):
    return lax.ppermute(x, "fsdp", places(shift_y, flip_z, flip_core))


def piece(at, dy, dz, flip_core=0):
    return ((at[0] + dy) % 4 * 2 + (at[1] + dz) % 2) * 2 + (at[2] + flip_core) % 2


class Program:

    def __init__(self, at):
        self.at = at
        self.last = []

    def call(self, body, name, ins, outs, grid=(1,), onto=None):
        operands, specs = map(list, zip(*ins))
        count = len(operands)
        extra = ([] if onto is None else [onto]) + self.last
        operands += extra
        specs += [pl.BlockSpec(memory_space=pl.ANY)] * len(extra)

        def kernel(at_ref, *refs):
            body(at_ref, *refs[:count], *refs[count + len(extra):])

        results = pl.pallas_call(
            kernel,
            grid_spec=pltpu.PrefetchScalarGridSpec(
                num_scalar_prefetch=1,
                grid=grid,
                in_specs=specs,
                out_specs=[spec for _, spec in outs],
            ),
            out_shape=[shape for shape, _ in outs],
            input_output_aliases={} if onto is None else {count + 1: 0},
            compiler_params=pltpu.CompilerParams(vmem_limit_bytes=VMEM),
            name=name,
        )(self.at, *operands)
        self.last = [results[-1]]
        return results


def whole(x):
    return x, pl.BlockSpec(x.shape, lambda s, at: (0,) * x.ndim)


HALF = 256
SENT = jnp.int16
VMEM = 10 * 1024 * 1024


STEP = 256


def local(partial_grads, momentum, freq_index):
    rows, cols = momentum.shape
    basis = jnp.asarray(dct_constants())
    pos = freq_index.reshape(rows // GROUP * (cols // WIDE), KEPT)
    me = lax.axis_index("fsdp")
    at = jnp.stack([me // 4, me // 2 % 2, me % 2]).astype(jnp.int32)
    groups = HALF // GROUP * (cols // WIDE)
    poss = [pos[i * groups:(i + 1) * groups] for i in range(rows // HALF)]
    places_sent = pos.astype(F32)
    program = Program(at)
    call = program.call
    quarter = jax.ShapeDtypeStruct((4, rows, cols), BF)

    def slab(dz, flip_core):
        return partial_grads, pl.BlockSpec((1, rows, cols), lambda s, at: (0, 0, piece(at, s, dz, flip_core)))

    def packed():
        return quarter, pl.BlockSpec((1, rows, cols), lambda s, at: (s, 0, 0))

    def out(height):
        shape = (height + (0 if SENT == F32 else PAD), cols)
        return jax.ShapeDtypeStruct(shape, SENT), pl.BlockSpec(shape, lambda s, at: (0, 0))

    def like(x):
        return jax.ShapeDtypeStruct(x.shape, x.dtype), whole(x)[1]

    own, sib = {}, {}
    other, = call(pack_kernel, "pack", [slab(1, 1)], [packed()], (4,))
    sib[1] = send(other, flip_core=1)
    other, own[1], own[0] = call(
        pack_kernel, "pack", [slab(0, 1), slab(1, 0), slab(0, 0)], [packed(), packed(), packed()], (4,))
    sib[0] = send(other, flip_core=1)

    def both(dz, dy, height=rows, i=0):
        spec = pl.BlockSpec((1, height, cols), lambda s, at: (dy % 4, i, 0))
        return [(own[dz], spec), (sib[dz], spec)]

    def round_y(x):
        return send(x[0], shift_y=1), send(x[1], shift_y=-1)

    far = {}
    for dz in (1, 0):
        far[dz] = round_y(call(far_kernel, "far", both(dz, 2), [out(HALF)] * 2))
        if dz:
            program.last += [places_sent, *poss]
    across_near = round_y(call(
        near_kernel, "near", both(1, 1) + both(1, -1) + [whole(far[1][0]), whole(far[1][1])], [out(rows)] * 2))
    program.last += far[0]
    *top, decayed, held = call(
        near_top_kernel, "near",
        both(0, 1, HALF, 0) + both(0, -1, HALF, 0) + [whole(far[0][0]), whole(momentum), whole(basis)],
        [out(HALF)] * 2 + [like(momentum), like(basis)])
    near = [round_y(top)]
    crossing = call(
        cross_kernel, "cross", both(1, 0) + [whole(across_near[0]), whole(across_near[1])], [out(HALF)] * 2)
    crossed = [send(x, flip_z=1) for x in crossing]
    near.append(round_y(call(
        near_low_kernel, "near", both(0, 1, HALF, 1) + both(0, -1, HALF, 1) + [whole(far[0][1])], [out(HALF)] * 2)))
    fresh, kept = None, places_sent
    for i in range(rows // HALF):
        height = kept.shape[0] + groups
        half_spec = pl.BlockSpec((HALF, cols), lambda s, at, i=i: (i, 0))
        fresh, kept = call(
            encode_kernel, "encode",
            [*both(0, 0, HALF, i), whole(near[i][0]), whole(near[i][1]), whole(crossed[i]), (decayed, half_spec),
             whole(poss[i]), whole(held), whole(kept)],
            [(jax.ShapeDtypeStruct((rows, cols), F32), half_spec),
             (jax.ShapeDtypeStruct((height, KEPT), F32), pl.BlockSpec((height, KEPT), lambda s, at: (0, 0)))],
            onto=fresh,
        )
    sent = along_z(kept)
    near_shape = (2 * (KEPT // K), pos.shape[0], KEPT)
    lines, = call(
        spread_kernel, "spread", [whole(x) for x in sent],
        [(jax.ShapeDtypeStruct(near_shape, F32), pl.BlockSpec(near_shape, lambda s, at: (0, 0, 0)))])
    sent = along_x(lines)
    spec = pl.BlockSpec((near_shape[0], STEP // GROUP * (cols // WIDE), KEPT), lambda s, at: (0, s, 0))
    update, = call(
        decode_kernel, "decode", [(x, spec) for x in sent] + [whole(held)],
        [(jax.ShapeDtypeStruct((rows, cols), F32), pl.BlockSpec((STEP, cols), lambda s, at: (s, 0)))],
        (rows // STEP,),
    )
    return fresh, update


def solution(mesh):
    return jax.shard_map(
        local,
        mesh=mesh,
        in_specs=(P(("rep", "fsdp"), None, None), P("rep", "fsdp"), P("rep", None, "fsdp", None)),
        out_specs=(P("rep", "fsdp"), P(None, "fsdp")),
        check_vma=False,
    )
```

```python
import functools

import jax
import jax.numpy as jnp
import numpy as np
from jax import lax
from jax.experimental import pallas as pl
from jax.experimental.pallas import tpu as pltpu
from jax.sharding import PartitionSpec as P

GROUP = 64
SHIFT = 6
K = 32
WIDE = 256
KEPT = 128
CHUNK = 128
DECAY = 0.9
BF = jnp.bfloat16
F32 = jnp.float32


def dct_constants():
    k = np.arange(GROUP)[:, None]
    n = np.arange(GROUP)[None, :]
    scale = np.where(k == 0, np.sqrt(1.0 / GROUP), np.sqrt(2.0 / GROUP))
    basis = scale * np.cos(np.pi * ((2 * n + 1) * k % (4 * GROUP)) / (2.0 * GROUP))
    wide = np.kron(np.eye(WIDE // GROUP), basis)
    both = np.stack([wide, wide.T]).astype(np.float32)
    high = both.astype(BF)
    low = (both - high.astype(np.float32)).astype(BF)
    return np.stack([high, low], axis=1)


def cut(x):
    high = x.astype(BF)
    return high, (x - high.astype(F32)).astype(BF)


def dot(a, b):
    return jnp.dot(a, b, preferred_element_type=F32)


def times_right(x, m_high, m_low):
    high, low = cut(x)
    return dot(high, m_high) + dot(high, m_low) + dot(low, m_high)


def times_left(m_high, m_low, x):
    high, low = cut(x)
    return dot(m_high, high) + dot(m_low, high) + dot(m_high, low)


def down_rows(m, x):
    step = min(x.shape[0], 2 * GROUP)
    high, low = m[0, :step, :step], m[1, :step, :step]
    parts = [times_left(high, low, x[i:i + step]) for i in range(0, x.shape[0], step)]
    return jnp.concatenate(parts, axis=0) if len(parts) > 1 else parts[0]


def forward(field, basis):
    return down_rows(basis[0], times_right(field, basis[1, 0], basis[1, 1]))


def inverse(coef, basis):
    return down_rows(basis[1], times_right(coef, basis[0, 0], basis[0, 1]))


def match(places, count):
    return lax.broadcasted_iota(jnp.int32, (count, places.shape[1]), 0) == places


def one(mask):
    return jnp.where(mask, F32(1.0), F32(0.0)).astype(BF)


def by_lanes(a, b):
    return lax.dot_general(a, b, (((1,), (1,)), ((), ())), preferred_element_type=F32)


def by_rows(a, b):
    return lax.dot_general(a, b, (((0,), (0,)), ((), ())), preferred_element_type=F32)


def encode(field, pos_ref, basis, fresh_ref, kept_ref):
    rows, cols = field.shape
    lane_block = lax.broadcasted_iota(jnp.int32, (1, KEPT), 1) // K
    row = pos_ref[...] >> SHIFT
    wide_col = (pos_ref[...] & (GROUP - 1)) + lane_block * GROUP
    for half in range(cols // WIDE):
        span = slice(half * WIDE, (half + 1) * WIDE)
        part = field[:, span]
        coef = forward(part, basis)
        dense = []
        for a in range(rows // GROUP):
            g = a * (cols // WIDE) + half
            block = coef[a * GROUP:(a + 1) * GROUP]
            on_col = match(wide_col[g:g + 1], WIDE)
            row_one = one(match(row[g:g + 1], GROUP))
            chosen = by_lanes(row_one, one(on_col))
            dense.append(jnp.where(chosen > 0.5, block, F32(0.0)))
            high, low = cut(block)
            rest = (block - high.astype(F32) - low.astype(F32)).astype(BF)
            three = jnp.concatenate([high, low, rest], axis=0)
            rows_of = by_rows(three, jnp.concatenate([row_one] * 3, axis=0))
            found = jnp.where(on_col, rows_of, F32(0.0))
            kept_ref[g:g + 1] = jnp.sum(found, axis=0, keepdims=True)
        fresh_ref[:, span] = part - inverse(jnp.concatenate(dense, axis=0), basis)


LEVELS = 32767.0
STEPS = 511.0
PAD = 16


def put(ref, x):
    if ref.dtype == F32:
        ref[...] = x
        return
    rows = x.shape[0]
    scale = jnp.maximum(jnp.ceil(jnp.max(jnp.abs(x), axis=0, keepdims=True) * STEPS), 1.0)
    ref[:rows] = jnp.round(x * (LEVELS * STEPS / scale)).astype(jnp.int32).astype(jnp.int16)
    ref[rows:] = jnp.broadcast_to(scale, (PAD, x.shape[1])).astype(jnp.int32).astype(jnp.int16)


def get(ref):
    if ref.dtype == F32:
        return ref[...]
    rows = ref.shape[0] - PAD
    scale = ref[rows:].astype(jnp.int32).astype(F32)[:1]
    return ref[:rows].astype(jnp.int32).astype(F32) * (scale * (1.0 / (LEVELS * STEPS)))


def wide(*refs):
    return sum(ref[0].astype(F32) for ref in refs)


def pack_kernel(at_ref, *refs):
    for i in range(len(refs) // 2):
        refs[len(refs) // 2 + i][...] = refs[i][...]


def far_kernel(at_ref, own, sib, up_ref, down_ref):
    x = wide(own, sib)
    put(up_ref, x[:HALF])
    put(down_ref, x[HALF:])


def near_kernel(at_ref, own_up, sib_up, own_down, sib_down, far_up, far_down, up_ref, down_ref):
    up, down = wide(own_up, sib_up), wide(own_down, sib_down)
    put(up_ref, jnp.concatenate([up[:HALF] + get(far_up), up[HALF:]], axis=0))
    put(down_ref, jnp.concatenate([down[:HALF], down[HALF:] + get(far_down)], axis=0))


def near_top_kernel(
    at_ref, own_up, sib_up, own_down, sib_down, far_up, own, sib, momentum, basis, up_ref, down_ref, started, held
):
    put(up_ref, wide(own_up, sib_up) + get(far_up))
    put(down_ref, wide(own_down, sib_down))
    started[...] = DECAY * momentum[...] + wide(own, sib)
    held[...] = basis[...]


def near_low_kernel(at_ref, own_up, sib_up, own_down, sib_down, far_down, up_ref, down_ref):
    put(up_ref, wide(own_up, sib_up))
    put(down_ref, wide(own_down, sib_down) + get(far_down))


def cross_kernel(at_ref, own, sib, up_ref, down_ref, top_ref, low_ref):
    x = wide(own, sib) + (get(up_ref) + get(down_ref))
    put(top_ref, x[:HALF])
    put(low_ref, x[HALF:])


def encode_kernel(at_ref, up_ref, down_ref, cross_ref, started_ref, pos_ref, basis_ref, *refs):
    *before, fresh_ref, kept_ref = refs
    field = started_ref[...] + (get(up_ref) + get(down_ref) + get(cross_ref))
    first = 0
    for ref in before:
        kept_ref[first:first + ref.shape[0]] = ref[...]
        first += ref.shape[0]
    encode(field, pos_ref, basis_ref, fresh_ref, kept_ref.at[first:])


def spread_kernel(at_ref, *refs):
    *sent, out_ref = refs
    lane_block = lax.broadcasted_iota(jnp.int32, (1, KEPT), 1) // K
    groups = out_ref.shape[1]
    for q in range(KEPT // K):
        total = None
        for s in range(2 * len(sent)):
            part = jnp.where(lane_block == q, sent[s // 2][s % 2], F32(0.0))
            shift = (s - q) * K % KEPT
            part = pltpu.roll(part, shift, 1) if shift else part
            total = part if total is None else total + part
        out_ref[2 * q] = total[:groups]
        out_ref[2 * q + 1] = total[groups:]


def decode_kernel(at_ref, *refs):
    *sent, basis, out_ref = refs
    halves = out_ref.shape[1] // WIDE
    parts = []
    for q in range(WIDE // GROUP):
        pos = jnp.concatenate([ref[2 * q] for ref in sent], axis=1).astype(jnp.int32)
        val = jnp.concatenate([ref[2 * q + 1] for ref in sent], axis=1)
        high = val.astype(BF).astype(F32)
        parts.append((pos >> SHIFT, pos & (GROUP - 1), high, val - high))
    for half in range(halves):
        lines = []
        for g in range(half, sent[0].shape[1], halves):
            dense = []
            for part in parts:
                row, col, high, low = [x[g:g + 1] for x in part]
                on_row = match(row, GROUP)
                left = [jnp.where(on_row, x, F32(0.0)).astype(BF) for x in (high, low)]
                both = by_lanes(jnp.concatenate(left, axis=0), one(match(col, GROUP)))
                dense.append(both[:GROUP] + both[GROUP:])
            lines.append(jnp.concatenate(dense, axis=1))
        out_ref[:, half * WIDE:(half + 1) * WIDE] = inverse(jnp.concatenate(lines, axis=0), basis)


def across(n_hi, n_x, shift_hi, shift_x):
    return [
        (h * n_x + x, (h + shift_hi) % n_hi * n_x + (x + shift_x) % n_x)
        for h in range(n_hi)
        for x in range(n_x)
    ]


def along_x(own):
    return [own] + [lax.ppermute(own, "rep", across(4, 4, 0, s)) for s in (1, 2, 3)]


def along_z(own):
    there = lax.ppermute(own, "rep", [(h * 4 + x, (h ^ 1) * 4 + x) for h in range(4) for x in range(4)])
    two = jnp.stack([own, there])
    return [two, lax.ppermute(two, "rep", [(h * 4 + x, (3 - h) * 4 + x) for h in range(4) for x in range(4)])]


def places(shift_y, flip_z, flip_core):
    return [
        ((y * 2 + z) * 2 + c, ((y + shift_y) % 4 * 2 + (z ^ flip_z)) * 2 + (c ^ flip_core))
        for y in range(4)
        for z in range(2)
        for c in range(2)
    ]


def send(x, shift_y=0, flip_z=0, flip_core=0):
    return lax.ppermute(x, "fsdp", places(shift_y, flip_z, flip_core))


def piece(at, dy, dz, flip_core=0):
    return ((at[0] + dy) % 4 * 2 + (at[1] + dz) % 2) * 2 + (at[2] + flip_core) % 2


class Program:

    def __init__(self, at):
        self.at = at
        self.last = []

    def call(self, body, name, ins, outs, grid=(1,), onto=None):
        operands, specs = map(list, zip(*ins))
        count = len(operands)
        extra = ([] if onto is None else [onto]) + self.last
        operands += extra
        specs += [pl.BlockSpec(memory_space=pl.ANY)] * len(extra)

        def kernel(at_ref, *refs):
            body(at_ref, *refs[:count], *refs[count + len(extra):])

        results = pl.pallas_call(
            kernel,
            grid_spec=pltpu.PrefetchScalarGridSpec(
                num_scalar_prefetch=1,
                grid=grid,
                in_specs=specs,
                out_specs=[spec for _, spec in outs],
            ),
            out_shape=[shape for shape, _ in outs],
            input_output_aliases={} if onto is None else {count + 1: 0},
            compiler_params=pltpu.CompilerParams(vmem_limit_bytes=VMEM),
            name=name,
        )(self.at, *operands)
        self.last = [results[-1]]
        return results


def whole(x):
    return x, pl.BlockSpec(x.shape, lambda s, at: (0,) * x.ndim)


HALF = 256
SENT = jnp.int16
VMEM = 10 * 1024 * 1024


STEP = 256


def local(partial_grads, momentum, freq_index):
    rows, cols = momentum.shape
    basis = jnp.asarray(dct_constants())
    pos = freq_index.reshape(rows // GROUP * (cols // WIDE), KEPT)
    me = lax.axis_index("fsdp")
    at = jnp.stack([me // 4, me // 2 % 2, me % 2]).astype(jnp.int32)
    groups = HALF // GROUP * (cols // WIDE)
    poss = [pos[i * groups:(i + 1) * groups] for i in range(rows // HALF)]
    places_sent = pos.astype(F32)
    program = Program(at)
    call = program.call
    quarter = jax.ShapeDtypeStruct((4, rows, cols), BF)

    def slab(dz, flip_core):
        return partial_grads, pl.BlockSpec((1, rows, cols), lambda s, at: (0, 0, piece(at, s, dz, flip_core)))

    def packed():
        return quarter, pl.BlockSpec((1, rows, cols), lambda s, at: (s, 0, 0))

    def out(height):
        shape = (height + (0 if SENT == F32 else PAD), cols)
        return jax.ShapeDtypeStruct(shape, SENT), pl.BlockSpec(shape, lambda s, at: (0, 0))

    def like(x):
        return jax.ShapeDtypeStruct(x.shape, x.dtype), whole(x)[1]

    own, sib = {}, {}
    other, = call(pack_kernel, "pack", [slab(1, 1)], [packed()], (4,))
    sib[1] = send(other, flip_core=1)
    other, own[1], own[0] = call(
        pack_kernel, "pack", [slab(0, 1), slab(1, 0), slab(0, 0)], [packed(), packed(), packed()], (4,))
    sib[0] = send(other, flip_core=1)

    def both(dz, dy, height=rows, i=0):
        spec = pl.BlockSpec((1, height, cols), lambda s, at: (dy % 4, i, 0))
        return [(own[dz], spec), (sib[dz], spec)]

    def round_y(x):
        return send(x[0], shift_y=1), send(x[1], shift_y=-1)

    far = {}
    for dz in (1, 0):
        far[dz] = round_y(call(far_kernel, "far", both(dz, 2), [out(HALF)] * 2))
        if dz:
            program.last += [places_sent, *poss]
    across_near = round_y(call(
        near_kernel, "near", both(1, 1) + both(1, -1) + [whole(far[1][0]), whole(far[1][1])], [out(rows)] * 2))
    program.last += far[0]
    *top, started, held = call(
        near_top_kernel, "near",
        both(0, 1, HALF, 0) + both(0, -1, HALF, 0) + [whole(far[0][0])] + both(0, 0) + [whole(momentum), whole(basis)],
        [out(HALF)] * 2 + [like(momentum), like(basis)])
    near = [round_y(top)]
    crossing = call(
        cross_kernel, "cross", both(1, 0) + [whole(across_near[0]), whole(across_near[1])], [out(HALF)] * 2)
    crossed = [send(x, flip_z=1) for x in crossing]
    near.append(round_y(call(
        near_low_kernel, "near", both(0, 1, HALF, 1) + both(0, -1, HALF, 1) + [whole(far[0][1])], [out(HALF)] * 2)))
    fresh, kept = None, places_sent
    for i in range(rows // HALF):
        height = kept.shape[0] + groups
        half_spec = pl.BlockSpec((HALF, cols), lambda s, at, i=i: (i, 0))
        fresh, kept = call(
            encode_kernel, "encode",
            [whole(near[i][0]), whole(near[i][1]), whole(crossed[i]), (started, half_spec),
             whole(poss[i]), whole(held), whole(kept)],
            [(jax.ShapeDtypeStruct((rows, cols), F32), half_spec),
             (jax.ShapeDtypeStruct((height, KEPT), F32), pl.BlockSpec((height, KEPT), lambda s, at: (0, 0)))],
            onto=fresh,
        )
    sent = along_z(kept)
    near_shape = (2 * (KEPT // K), pos.shape[0], KEPT)
    lines, = call(
        spread_kernel, "spread", [whole(x) for x in sent],
        [(jax.ShapeDtypeStruct(near_shape, F32), pl.BlockSpec(near_shape, lambda s, at: (0, 0, 0)))])
    sent = along_x(lines)
    spec = pl.BlockSpec((near_shape[0], STEP // GROUP * (cols // WIDE), KEPT), lambda s, at: (0, s, 0))
    update, = call(
        decode_kernel, "decode", [(x, spec) for x in sent] + [whole(held)],
        [(jax.ShapeDtypeStruct((rows, cols), F32), pl.BlockSpec((STEP, cols), lambda s, at: (s, 0)))],
        (rows // STEP,),
    )
    return fresh, update


def solution(mesh):
    return jax.shard_map(
        local,
        mesh=mesh,
        in_specs=(P(("rep", "fsdp"), None, None), P("rep", "fsdp"), P("rep", None, "fsdp", None)),
        out_specs=(P("rep", "fsdp"), P(None, "fsdp")),
        check_vma=False,
    )
```

```python
import functools

import jax
import jax.numpy as jnp
import numpy as np
from jax import lax
from jax.experimental import pallas as pl
from jax.experimental.pallas import tpu as pltpu
from jax.sharding import PartitionSpec as P

GROUP = 64
SHIFT = 6
K = 32
WIDE = 256
KEPT = 128
CHUNK = 128
DECAY = 0.9
BF = jnp.bfloat16
F32 = jnp.float32


def dct_constants():
    k = np.arange(GROUP)[:, None]
    n = np.arange(GROUP)[None, :]
    scale = np.where(k == 0, np.sqrt(1.0 / GROUP), np.sqrt(2.0 / GROUP))
    basis = scale * np.cos(np.pi * ((2 * n + 1) * k % (4 * GROUP)) / (2.0 * GROUP))
    wide = np.kron(np.eye(WIDE // GROUP), basis)
    both = np.stack([wide, wide.T]).astype(np.float32)
    high = both.astype(BF)
    low = (both - high.astype(np.float32)).astype(BF)
    return np.stack([high, low], axis=1)


def cut(x):
    high = x.astype(BF)
    return high, (x - high.astype(F32)).astype(BF)


def dot(a, b):
    return jnp.dot(a, b, preferred_element_type=F32)


def times_right(x, m_high, m_low):
    high, low = cut(x)
    return dot(high, m_high) + dot(high, m_low) + dot(low, m_high)


def times_left(m_high, m_low, x):
    high, low = cut(x)
    return dot(m_high, high) + dot(m_low, high) + dot(m_high, low)


def down_rows(m, x):
    step = min(x.shape[0], 2 * GROUP)
    high, low = m[0, :step, :step], m[1, :step, :step]
    parts = [times_left(high, low, x[i:i + step]) for i in range(0, x.shape[0], step)]
    return jnp.concatenate(parts, axis=0) if len(parts) > 1 else parts[0]


def forward(field, basis):
    return down_rows(basis[0], times_right(field, basis[1, 0], basis[1, 1]))


def inverse(coef, basis):
    return down_rows(basis[1], times_right(coef, basis[0, 0], basis[0, 1]))


def match(places, count):
    return lax.broadcasted_iota(jnp.int32, (count, places.shape[1]), 0) == places


def one(mask):
    return jnp.where(mask, F32(1.0), F32(0.0)).astype(BF)


def by_lanes(a, b):
    return lax.dot_general(a, b, (((1,), (1,)), ((), ())), preferred_element_type=F32)


def by_rows(a, b):
    return lax.dot_general(a, b, (((0,), (0,)), ((), ())), preferred_element_type=F32)


def encode(field, pos_ref, basis, fresh_ref, kept_ref):
    rows, cols = field.shape
    lane_block = lax.broadcasted_iota(jnp.int32, (1, KEPT), 1) // K
    row = pos_ref[...] >> SHIFT
    wide_col = (pos_ref[...] & (GROUP - 1)) + lane_block * GROUP
    for half in range(cols // WIDE):
        span = slice(half * WIDE, (half + 1) * WIDE)
        part = field[:, span]
        coef = forward(part, basis)
        dense = []
        for a in range(rows // GROUP):
            g = a * (cols // WIDE) + half
            block = coef[a * GROUP:(a + 1) * GROUP]
            on_col = match(wide_col[g:g + 1], WIDE)
            row_one = one(match(row[g:g + 1], GROUP))
            chosen = by_lanes(row_one, one(on_col))
            dense.append(jnp.where(chosen > 0.5, block, F32(0.0)))
            high, low = cut(block)
            rest = (block - high.astype(F32) - low.astype(F32)).astype(BF)
            three = jnp.concatenate([high, low, rest], axis=0)
            rows_of = by_rows(three, jnp.concatenate([row_one] * 3, axis=0))
            found = jnp.where(on_col, rows_of, F32(0.0))
            kept_ref[g:g + 1] = jnp.sum(found, axis=0, keepdims=True)
        fresh_ref[:, span] = part - inverse(jnp.concatenate(dense, axis=0), basis)


LEVELS = 32767.0
STEPS = 511.0
PAD = 16


def put(ref, x):
    if ref.dtype == F32:
        ref[...] = x
        return
    rows = x.shape[0]
    scale = jnp.maximum(jnp.ceil(jnp.max(jnp.abs(x), axis=0, keepdims=True) * STEPS), 1.0)
    ref[:rows] = jnp.round(x * (LEVELS * STEPS / scale)).astype(jnp.int32).astype(jnp.int16)
    ref[rows:] = jnp.broadcast_to(scale, (PAD, x.shape[1])).astype(jnp.int32).astype(jnp.int16)


def get(ref):
    if ref.dtype == F32:
        return ref[...]
    rows = ref.shape[0] - PAD
    scale = ref[rows:].astype(jnp.int32).astype(F32)[:1]
    return ref[:rows].astype(jnp.int32).astype(F32) * (scale * (1.0 / (LEVELS * STEPS)))


def wide(*refs):
    return sum(ref[0].astype(F32) for ref in refs)


def pack_kernel(at_ref, *refs):
    for i in range(len(refs) // 2):
        refs[len(refs) // 2 + i][...] = refs[i][...]


def far_kernel(at_ref, own, sib, up_ref, down_ref):
    x = wide(own, sib)
    put(up_ref, x[:HALF])
    put(down_ref, x[HALF:])


def near_kernel(at_ref, own_up, sib_up, own_down, sib_down, far_up, far_down, up_ref, down_ref):
    up, down = wide(own_up, sib_up), wide(own_down, sib_down)
    put(up_ref, jnp.concatenate([up[:HALF] + get(far_up), up[HALF:]], axis=0))
    put(down_ref, jnp.concatenate([down[:HALF], down[HALF:] + get(far_down)], axis=0))


def near_top_kernel(
    at_ref, own_up, sib_up, own_down, sib_down, far_up, own, sib, momentum, basis, up_ref, down_ref, started, held
):
    put(up_ref, wide(own_up, sib_up) + get(far_up))
    put(down_ref, wide(own_down, sib_down))
    started[...] = DECAY * momentum[...] + wide(own, sib)
    held[...] = basis[...]


def near_low_kernel(at_ref, own_up, sib_up, own_down, sib_down, far_down, up_ref, down_ref):
    put(up_ref, wide(own_up, sib_up))
    put(down_ref, wide(own_down, sib_down) + get(far_down))


def cross_kernel(at_ref, own, sib, up_ref, down_ref, top_ref, low_ref):
    x = wide(own, sib) + (get(up_ref) + get(down_ref))
    put(top_ref, x[:HALF])
    put(low_ref, x[HALF:])


def encode_kernel(at_ref, up_ref, down_ref, cross_ref, started_ref, pos_ref, basis_ref, *refs):
    *before, fresh_ref, kept_ref = refs
    field = started_ref[...] + (get(up_ref) + get(down_ref) + get(cross_ref))
    first = 0
    for ref in before:
        kept_ref[first:first + ref.shape[0]] = ref[...]
        first += ref.shape[0]
    encode(field, pos_ref, basis_ref, fresh_ref, kept_ref.at[first:])


def spread_kernel(at_ref, *refs):
    *sent, out_ref = refs
    lane_block = lax.broadcasted_iota(jnp.int32, (1, KEPT), 1) // K
    groups = out_ref.shape[1]
    for q in range(KEPT // K):
        total = None
        for s in range(2 * len(sent)):
            part = jnp.where(lane_block == q, sent[s // 2][s % 2], F32(0.0))
            shift = (s - q) * K % KEPT
            part = pltpu.roll(part, shift, 1) if shift else part
            total = part if total is None else total + part
        out_ref[2 * q] = total[:groups]
        out_ref[2 * q + 1] = total[groups:]


def decode_kernel(at_ref, *refs):
    *sent, basis, out_ref = refs
    halves = out_ref.shape[1] // WIDE
    parts = []
    for q in range(WIDE // GROUP):
        pos = jnp.concatenate([ref[2 * q] for ref in sent], axis=1).astype(jnp.int32)
        val = jnp.concatenate([ref[2 * q + 1] for ref in sent], axis=1)
        high = val.astype(BF).astype(F32)
        parts.append((pos >> SHIFT, pos & (GROUP - 1), high, val - high))
    for half in range(halves):
        lines = []
        for g in range(half, sent[0].shape[1], halves):
            dense = []
            for part in parts:
                row, col, high, low = [x[g:g + 1] for x in part]
                on_row = match(row, GROUP)
                left = [jnp.where(on_row, x, F32(0.0)).astype(BF) for x in (high, low)]
                both = by_lanes(jnp.concatenate(left, axis=0), one(match(col, GROUP)))
                dense.append(both[:GROUP] + both[GROUP:])
            lines.append(jnp.concatenate(dense, axis=1))
        out_ref[:, half * WIDE:(half + 1) * WIDE] = inverse(jnp.concatenate(lines, axis=0), basis)


def across(n_hi, n_x, shift_hi, shift_x):
    return [
        (h * n_x + x, (h + shift_hi) % n_hi * n_x + (x + shift_x) % n_x)
        for h in range(n_hi)
        for x in range(n_x)
    ]


def along_x(own):
    return [own] + [lax.ppermute(own, "rep", across(4, 4, 0, s)) for s in (1, 2, 3)]


def along_z(own):
    there = lax.ppermute(own, "rep", [(h * 4 + x, (h ^ 1) * 4 + x) for h in range(4) for x in range(4)])
    two = jnp.stack([own, there])
    return [two, lax.ppermute(two, "rep", [(h * 4 + x, (3 - h) * 4 + x) for h in range(4) for x in range(4)])]


def places(shift_y, flip_z, flip_core):
    return [
        ((y * 2 + z) * 2 + c, ((y + shift_y) % 4 * 2 + (z ^ flip_z)) * 2 + (c ^ flip_core))
        for y in range(4)
        for z in range(2)
        for c in range(2)
    ]


def send(x, shift_y=0, flip_z=0, flip_core=0):
    return lax.ppermute(x, "fsdp", places(shift_y, flip_z, flip_core))


def piece(at, dy, dz, flip_core=0):
    return ((at[0] + dy) % 4 * 2 + (at[1] + dz) % 2) * 2 + (at[2] + flip_core) % 2


class Program:

    def __init__(self, at):
        self.at = at
        self.last = []

    def call(self, body, name, ins, outs, grid=(1,), onto=None):
        operands, specs = map(list, zip(*ins))
        count = len(operands)
        extra = ([] if onto is None else [onto]) + self.last
        operands += extra
        specs += [pl.BlockSpec(memory_space=pl.ANY)] * len(extra)

        def kernel(at_ref, *refs):
            body(at_ref, *refs[:count], *refs[count + len(extra):])

        results = pl.pallas_call(
            kernel,
            grid_spec=pltpu.PrefetchScalarGridSpec(
                num_scalar_prefetch=1,
                grid=grid,
                in_specs=specs,
                out_specs=[spec for _, spec in outs],
            ),
            out_shape=[shape for shape, _ in outs],
            input_output_aliases={} if onto is None else {count + 1: 0},
            compiler_params=pltpu.CompilerParams(vmem_limit_bytes=VMEM),
            name=name,
        )(self.at, *operands)
        self.last = [results[-1]]
        return results


def whole(x):
    return x, pl.BlockSpec(x.shape, lambda s, at: (0,) * x.ndim)


HALF = 256
SENT = jnp.int16
VMEM = 10 * 1024 * 1024


STEP = 512


def local(partial_grads, momentum, freq_index):
    rows, cols = momentum.shape
    basis = jnp.asarray(dct_constants())
    pos = freq_index.reshape(rows // GROUP * (cols // WIDE), KEPT)
    me = lax.axis_index("fsdp")
    at = jnp.stack([me // 4, me // 2 % 2, me % 2]).astype(jnp.int32)
    groups = HALF // GROUP * (cols // WIDE)
    poss = [pos[i * groups:(i + 1) * groups] for i in range(rows // HALF)]
    places_sent = pos.astype(F32)
    program = Program(at)
    call = program.call
    quarter = jax.ShapeDtypeStruct((4, rows, cols), BF)

    def slab(dz, flip_core):
        return partial_grads, pl.BlockSpec((1, rows, cols), lambda s, at: (0, 0, piece(at, s, dz, flip_core)))

    def packed():
        return quarter, pl.BlockSpec((1, rows, cols), lambda s, at: (s, 0, 0))

    def out(height):
        shape = (height + (0 if SENT == F32 else PAD), cols)
        return jax.ShapeDtypeStruct(shape, SENT), pl.BlockSpec(shape, lambda s, at: (0, 0))

    def like(x):
        return jax.ShapeDtypeStruct(x.shape, x.dtype), whole(x)[1]

    own, sib = {}, {}
    other, = call(pack_kernel, "pack", [slab(1, 1)], [packed()], (4,))
    sib[1] = send(other, flip_core=1)
    other, own[1], own[0] = call(
        pack_kernel, "pack", [slab(0, 1), slab(1, 0), slab(0, 0)], [packed(), packed(), packed()], (4,))
    sib[0] = send(other, flip_core=1)

    def both(dz, dy, height=rows, i=0):
        spec = pl.BlockSpec((1, height, cols), lambda s, at: (dy % 4, i, 0))
        return [(own[dz], spec), (sib[dz], spec)]

    def round_y(x):
        return send(x[0], shift_y=1), send(x[1], shift_y=-1)

    far = {}
    for dz in (1, 0):
        far[dz] = round_y(call(far_kernel, "far", both(dz, 2), [out(HALF)] * 2))
        if dz:
            program.last += [places_sent, *poss]
    across_near = round_y(call(
        near_kernel, "near", both(1, 1) + both(1, -1) + [whole(far[1][0]), whole(far[1][1])], [out(rows)] * 2))
    program.last += far[0]
    *top, started, held = call(
        near_top_kernel, "near",
        both(0, 1, HALF, 0) + both(0, -1, HALF, 0) + [whole(far[0][0])] + both(0, 0) + [whole(momentum), whole(basis)],
        [out(HALF)] * 2 + [like(momentum), like(basis)])
    near = [round_y(top)]
    crossing = call(
        cross_kernel, "cross", both(1, 0) + [whole(across_near[0]), whole(across_near[1])], [out(HALF)] * 2)
    crossed = [send(x, flip_z=1) for x in crossing]
    near.append(round_y(call(
        near_low_kernel, "near", both(0, 1, HALF, 1) + both(0, -1, HALF, 1) + [whole(far[0][1])], [out(HALF)] * 2)))
    fresh, kept = None, places_sent
    for i in range(rows // HALF):
        height = kept.shape[0] + groups
        half_spec = pl.BlockSpec((HALF, cols), lambda s, at, i=i: (i, 0))
        fresh, kept = call(
            encode_kernel, "encode",
            [whole(near[i][0]), whole(near[i][1]), whole(crossed[i]), (started, half_spec),
             whole(poss[i]), whole(held), whole(kept)],
            [(jax.ShapeDtypeStruct((rows, cols), F32), half_spec),
             (jax.ShapeDtypeStruct((height, KEPT), F32), pl.BlockSpec((height, KEPT), lambda s, at: (0, 0)))],
            onto=fresh,
        )
    sent = along_z(kept)
    near_shape = (2 * (KEPT // K), pos.shape[0], KEPT)
    lines, = call(
        spread_kernel, "spread", [whole(x) for x in sent],
        [(jax.ShapeDtypeStruct(near_shape, F32), pl.BlockSpec(near_shape, lambda s, at: (0, 0, 0)))])
    sent = along_x(lines)
    spec = pl.BlockSpec((near_shape[0], STEP // GROUP * (cols // WIDE), KEPT), lambda s, at: (0, s, 0))
    update, = call(
        decode_kernel, "decode", [(x, spec) for x in sent] + [whole(held)],
        [(jax.ShapeDtypeStruct((rows, cols), F32), pl.BlockSpec((STEP, cols), lambda s, at: (s, 0)))],
        (rows // STEP,),
    )
    return fresh, update


def solution(mesh):
    return jax.shard_map(
        local,
        mesh=mesh,
        in_specs=(P(("rep", "fsdp"), None, None), P("rep", "fsdp"), P("rep", None, "fsdp", None)),
        out_specs=(P("rep", "fsdp"), P(None, "fsdp")),
        check_vma=False,
    )
```
